32 devices in a mesh: cfg: 2 (over x), space: 16 (over z, y, core).
Axes of the slice: x: 2, y: 2, z: 4, core: 2. Of those that a mesh axis runs over, the one named last changes fastest.
Arguments:
- vectors: float32 [4, 2, 3, 2048, 256], P('cfg', None, None, 'space'), parts along dimension 0, may hold values from -1.75 to 1.75
- links: float32 [4, 3, 2, 3, 3, 2048], P('cfg', None, None, None, None, 'space'), parts along dimension 0, may hold values from -2.5 to 2.5
- directions: int32 [3], replicated, may hold values from 0 to 2
- slice_group: int32 [2], replicated, may hold values from 0 to 1, as said below
- peram: float32 [4, 1024, 1024], P('cfg', None, 'space'), parts along dimension 0, may hold values from -0.3125 to 0.3125
- block_group: int32 [16], P('space'), may hold values from 0 to 1
Outputs:
- elementals: float32 [4, 3, 2, 256, 256], P('cfg', None, None, 'space'), parts along dimension 0
- blocks: float32 [4, 1024, 64], P('cfg', 'space'), parts along dimension 0
The draws below stay inside these ranges and needn't reach their ends.
There are 2 independent parts, one for each index of `cfg`. The reference program is written for one: setup_inputs(seed, part) draws one part's arguments, and reference() takes and returns one part's arrays. A program takes and returns all parts, laid end to end along the dimension named above; an argument that names none is the same for every part. Nothing has to cross between parts.
Inputs may be any that keep to these rules, and one draw needn't show every extreme that they name: `slice_group`: every group holds at least one timeslice.
All inputs are finite; a program needn't handle non-finite values.
Results may differ from the reference program's by a relative error of at most 0.0001.
Values sent between devices are 32-bit elements; how exact they have to be, the bound alone decides.
A program may use at most 64 MiB of HBM per device.

```python
import jax
import jax.numpy as jnp
import numpy as np
from jax import lax

NV = 256
NT = 2
NG = 2
LY = 16
LZ = 16
LX = 8
SITES = 2048
CB = 64
N_SPACE = 16


def draw_slice_group(key, part):
    group_key, order_key = jax.random.split(jax.random.fold_in(key, 11))
    base = jax.random.randint(group_key, (NT,), 0, NG, dtype=jnp.int32)
    order = jax.random.permutation(order_key, jnp.arange(NT, dtype=jnp.int32))
    return base.at[order[:NG]].set(jnp.arange(NG, dtype=jnp.int32))


def with_ends(entries, rng, smallest, largest):
    longest = entries.shape.index(max(entries.shape))
    spots = []
    for shift in (0, 1):
        where = [jax.random.randint(jax.random.fold_in(rng, axis), (), 0, length) for axis, length in enumerate(entries.shape)]
        where[longest] = (where[longest] + shift) % entries.shape[longest]
        spots.append(tuple(where))
    return entries.at[spots[0]].set(smallest).at[spots[1]].set(largest)


def shard_levels(own_key, shape, pieces, least, top_value):
    loudness, own = 1.0, jax.random.fold_in(own_key, 6)
    for dim, parts in pieces:
        steps = jnp.exp(jax.random.uniform(jax.random.fold_in(own, dim), (parts,), jnp.float32, least / len(pieces), top_value / len(pieces)))
        loudness = loudness * jnp.repeat(steps, shape[dim] // parts).reshape([-1 if axis == dim else 1 for axis in range(len(shape))])
    return loudness


def scatter_about(rng, shape, scale, limit, cuts=(), held_as=jnp.bfloat16):
    factor_of = shard_levels(rng, shape, cuts, -0.22, 0.18) if cuts else 1.0
    result = jax.random.normal(rng, shape, jnp.float32) * scale * factor_of
    return jnp.minimum(jnp.maximum(result, -limit), limit).astype(held_as)


def setup_inputs(seed: int = 0, part: int = 0) -> dict:
    key_list = jax.random.split(jax.random.key(seed), 7)
    own_keys = jax.random.split(jax.random.fold_in(key_list[6], part), 7)
    vectors = scatter_about(own_keys[0], (NT, 2, 3, SITES, NV), ((3 * SITES) ** -0.25), 1.75, ((3, 16),), jnp.float32)
    links = scatter_about(own_keys[1], (NT, 3, 2, 3, 3, SITES), 6 ** -0.5, 2.5, ((5, 16),), jnp.float32)
    directions = jax.random.randint(key_list[2], (3,), 0, 3).astype(jnp.int32)
    slice_group = draw_slice_group(jax.random.fold_in(key_list[6], 71), part)
    peram = scatter_about(own_keys[4], (2, 4 * NV, 4 * NV), ((8 * NV) ** -0.5), 0.3125, ((2, 16),), jnp.float32)
    block_group = with_ends(jax.random.randint(key_list[5], (N_SPACE,), 0, NG), jax.random.fold_in(key_list[5], 1), 0, NG - 1).astype(jnp.int32)
    return dict(vectors=vectors, links=links, directions=directions, slice_group=slice_group, peram=peram, block_group=block_group)


precise = lax.Precision.HIGHEST


def gamma_tables():
    pauli_one = np.array([[0.0, 1.0], [1.0, 0.0]])
    pauli_three = np.array([[1.0, 0.0], [0.0, -1.0]])
    rotate = np.array([[0.0, -1.0], [1.0, 0.0]])
    real_part = np.zeros((3, 4, 4))
    imag_part = np.zeros((3, 4, 4))
    imag_part[0, :2, 2:] = -pauli_one
    imag_part[0, 2:, :2] = pauli_one
    real_part[1, :2, 2:] = rotate
    real_part[1, 2:, :2] = -rotate
    imag_part[2, :2, 2:] = -pauli_three
    imag_part[2, 2:, :2] = pauli_three
    return jnp.asarray(real_part, jnp.float32), jnp.asarray(imag_part, jnp.float32)


def apply_link(matrix, vector_field):
    link_real = matrix[0][..., None]
    link_imag = matrix[1][..., None]
    vec_real = vector_field[0][None]
    vec_imag = vector_field[1][None]
    real_part = jnp.sum(link_real * vec_real - link_imag * vec_imag, axis=1)
    imag_part = jnp.sum(link_real * vec_imag + link_imag * vec_real, axis=1)
    return jnp.stack([real_part, imag_part])


def apply_adjoint(matrix, vector_field):
    link_real = jnp.swapaxes(matrix[0], 0, 1)[..., None]
    link_imag = jnp.swapaxes(matrix[1], 0, 1)[..., None]
    vec_real = vector_field[0][None]
    vec_imag = vector_field[1][None]
    real_part = jnp.sum(link_real * vec_real + link_imag * vec_imag, axis=1)
    imag_part = jnp.sum(link_real * vec_imag - link_imag * vec_real, axis=1)
    return jnp.stack([real_part, imag_part])


def contract(vector_field, derived):
    width = vector_field.shape[-1]
    left_rows = vector_field.reshape(-1, width)
    right_real = derived.reshape(-1, width)
    right_imag = jnp.stack([derived[1], -derived[0]]).reshape(-1, width)
    real_part = jnp.einsum("kv,kw->vw", left_rows, right_real, precision=precise)
    imag_part = jnp.einsum("kv,kw->vw", left_rows, right_imag, precision=precise)
    return jnp.stack([real_part, imag_part])


def reference(vectors, links, directions, slice_group, peram, block_group):
    field_all = vectors.reshape(NT, 2, 3, LX, LY, LZ, NV)
    gauge_all = links.reshape(NT, 3, 2, 3, 3, LX, LY, LZ)
    per_time = []
    for tslice in range(NT):
        eigen_field = field_all[tslice]
        elem_terms = []
        for axis_index in range(3):
            matrix = gauge_all[tslice, axis_index]
            ahead_field = jnp.roll(eigen_field, -1, axis=2 + axis_index)
            behind = jnp.roll(apply_adjoint(matrix, eigen_field), 1, axis=2 + axis_index)
            derived = 0.5 * (apply_link(matrix, ahead_field) - behind)
            elem_terms.append(contract(eigen_field, derived))
        per_time.append(jnp.stack(elem_terms))
    by_direction = jnp.stack(per_time)
    direction_hot = (directions[:, None] == jnp.arange(3, dtype=jnp.int32)[None, :]).astype(jnp.float32)
    chosen = jnp.einsum("ki,tirvw->tkrvw", direction_hot, by_direction, precision=precise)
    group_hot = (slice_group[:, None] == jnp.arange(NG, dtype=jnp.int32)[None, :]).astype(jnp.float32)
    elementals = jnp.einsum("tg,tkrvw->gkrvw", group_hot, chosen, precision=precise)
    gamma_real, gamma_imag = gamma_tables()
    col_blocks = peram.reshape(2, 4, NV, N_SPACE, CB)
    peram_real = col_blocks[0]
    peram_imag = col_blocks[1]
    block_hot = (block_group[:, None] == jnp.arange(NG, dtype=jnp.int32)[None, :]).astype(jnp.float32)
    picked = jnp.einsum("jg,gkrvw->jkrvw", block_hot, elementals, precision=precise)
    elem_real = picked[:, :, 0]
    elem_imag = picked[:, :, 1]
    mid_real = (jnp.einsum("jkvw,swjc->jksvc", elem_real, peram_real, precision=precise)
                - jnp.einsum("jkvw,swjc->jksvc", elem_imag, peram_imag, precision=precise))
    mid_imag = (jnp.einsum("jkvw,swjc->jksvc", elem_real, peram_imag, precision=precise)
                + jnp.einsum("jkvw,swjc->jksvc", elem_imag, peram_real, precision=precise))
    out_real = (jnp.einsum("kab,jkbvc->javc", gamma_real, mid_real, precision=precise)
                - jnp.einsum("kab,jkbvc->javc", gamma_imag, mid_imag, precision=precise))
    out_imag = (jnp.einsum("kab,jkbvc->javc", gamma_real, mid_imag, precision=precise)
                + jnp.einsum("kab,jkbvc->javc", gamma_imag, mid_real, precision=precise))
    res_real = (jnp.einsum("avjc,javd->jcd", peram_real, out_real, precision=precise)
                + jnp.einsum("avjc,javd->jcd", peram_imag, out_imag, precision=precise))
    res_imag = (jnp.einsum("avjc,javd->jcd", peram_real, out_imag, precision=precise)
                - jnp.einsum("avjc,javd->jcd", peram_imag, out_real, precision=precise))
    blocks = jnp.stack([res_real, res_imag]).reshape(2, N_SPACE * CB, CB)
    return elementals, blocks
```

```python
import functools

import jax
import jax.numpy as jnp
from jax import lax
from jax.experimental import pallas as pl
from jax.experimental.pallas import tpu as pltpu
from jax.sharding import PartitionSpec as P

NG = 2
LZ = 16
MESH = pl.DeviceIdType.MESH
precise = lax.Precision.HIGHEST
f32 = jnp.float32
bf16 = jnp.bfloat16


def split(value):
    high = value.astype(bf16)
    return high, (value - high.astype(f32)).astype(bf16)


def kernel(
    n, vec, lnk, per, dirs, sgroup, bgroup, elem, blocks,
    pvec, zvec, edge, plnk, zlnk, ut, lth, ltl, xh, xl, acc, part, recv, full, tcol,
    rhsh, rhsl, send_sem, recv_sem,
):
    sites = vec.shape[3]
    nv = vec.shape[4]
    cb = per.shape[2]
    rl = nv // n
    me = lax.axis_index("space")
    cfg = lax.axis_index("cfg")
    core = lax.rem(me, 2)
    b = lax.rem(me // 2, 2)

    def flip(mask):
        return me + mask * (1 - 2 * lax.rem(me // mask, 2))

    up = lax.rem(me + 4, n)
    down = lax.rem(me + n - 4, n)
    zmasks = []
    mask = 4
    while mask < n:
        zmasks.append(mask)
        mask *= 2
    others = [flip(1), flip(2), up, down] + [flip(m) for m in zmasks]
    barrier = pltpu.get_barrier_semaphore()
    for other in others:
        pl.semaphore_signal(barrier, inc=1, device_id=(cfg, other), device_id_type=MESH)
    pl.semaphore_wait(barrier, len(others))

    used = [0]

    def send(src, dst, other):
        i = used[0]
        used[0] += 1
        copy = pltpu.make_async_remote_copy(
            src_ref=src, dst_ref=dst, send_sem=send_sem.at[i], recv_sem=recv_sem.at[i],
            device_id=(cfg, other), device_id_type=MESH,
        )
        copy.start()
        return copy

    partner, mate = flip(2), flip(1)
    zdst = lax.rem(me + n + 8 * b - 4, n)
    got_edge = send(vec.at[b, :, :, pl.ds(0, LZ), :], edge.at[0], mate)
    got_plnk = send(lnk.at[1 - b], plnk, partner)
    got_zlnk = send(lnk.at[b], zlnk, zdst)
    got_pvec = send(vec.at[1 - b], pvec, partner)
    got_zvec = send(vec.at[b], zvec, zdst)

    def set_left(get):
        for ri in range(2):
            for c in range(3):
                j = ri * 3 + c
                high, low = split(jnp.transpose(get(ri, c)))
                lth[:, j * sites:(j + 1) * sites] = high
                ltl[:, j * sites:(j + 1) * sites] = low

    step = 16

    def derive(slot, column, fetch):
        def chunk(q, carry):
            base = pl.multiple_of(q * step, step)
            rows = pl.ds(base, step)
            link = ut[slot, rows, :]
            out_r = [None] * 3
            out_i = [None] * 3
            for c in range(3):
                vr = fetch(0, c, q, base)
                vi = fetch(1, c, q, base)
                for r in range(3):
                    j = column + r * 3 + c
                    lr = jnp.broadcast_to(link[:, j:j + 1], (step, nv))
                    li = jnp.broadcast_to(link[:, j + 9:j + 10], (step, nv))
                    tr = lr * vr - li * vi
                    ti = lr * vi + li * vr
                    out_r[r] = tr if c == 0 else out_r[r] + tr
                    out_i[r] = ti if c == 0 else out_i[r] + ti
            for r in range(3):
                plus = out_r[r] + out_i[r]
                minus = out_i[r] - out_r[r]
                ph, plo = split(plus)
                mh, mlo = split(minus)
                first = pl.ds(pl.multiple_of(r * sites + base, step), step)
                second = pl.ds(pl.multiple_of((3 + r) * sites + base, step), step)
                xh[first, :nv] = ph
                xl[first, :nv] = plo
                xh[second, :nv] = mh
                xl[second, :nv] = mlo
                xh[first, nv:] = mh
                xl[first, nv:] = mlo
                xh[second, nv:] = -ph
                xl[second, nv:] = -plo
            return carry

        lax.fori_loop(0, sites // step, chunk, 0)

    def contract(direction, first):
        prod = jnp.dot(lth[...], xh[...], preferred_element_type=f32)
        prod += jnp.dot(lth[...], xl[...], preferred_element_type=f32)
        prod += jnp.dot(ltl[...], xh[...], preferred_element_type=f32)
        if first:
            acc[direction] = prod
        else:
            acc[direction] += prod

    def set_links(slot, rows):
        ut[slot] = jnp.transpose(rows)

    def fetch_plain(get):
        return lambda ri, c, q, base: get(ri, c, pl.ds(base, step))

    def fetch_z(get):
        def fetch(ri, c, q, base):
            block = get(ri, c, pl.ds(base, step))
            return jnp.concatenate([block[1:], block[:1]], axis=0)
        return fetch

    def fetch_y(get, k):
        count = sites // LZ

        def fetch(ri, c, q, base):
            start = pl.multiple_of(lax.rem(q + 1, count) * step, step)
            inner = get(ri, c, pl.ds(start, step))
            return jnp.where(q == count - 1, edge[k, ri, c], inner)
        return fetch

    def own(ri, c, rows):
        return vec[b, ri, c, rows, :]

    def theirs(ri, c, rows):
        return pvec[ri, c, rows, :]

    def beyond(ri, c, rows):
        return zvec[ri, c, rows, :]

    everything = pl.ds(0, sites)
    set_left(lambda ri, c: own(ri, c, everything))
    set_links(0, lnk[b])
    derive(0, 36, fetch_z(own))
    contract(2, True)
    got_edge.wait()
    derive(0, 18, fetch_y(own, 0))
    contract(1, True)

    lo = [[per[ri, (2 + s) * nv:(3 + s) * nv, :] for ri in range(2)] for s in range(2)]
    turned = [
        [lo[1], lo[0]],
        [[lo[1][1], -lo[1][0]], [-lo[0][1], lo[0][0]]],
        [lo[0], [-lo[1][0], -lo[1][1]]],
    ]
    for k in range(3):
        (ar, ai), (br, bi) = turned[k]
        high, low = split(jnp.concatenate([ar, br, ai, bi], axis=1))
        rhsh[2 * k * nv:(2 * k + 1) * nv, :] = high
        rhsl[2 * k * nv:(2 * k + 1) * nv, :] = low
        high, low = split(jnp.concatenate([-ai, -bi, ar, br], axis=1))
        rhsh[(2 * k + 1) * nv:(2 * k + 2) * nv, :] = high
        rhsl[(2 * k + 1) * nv:(2 * k + 2) * nv, :] = low

    got_plnk.wait()
    got_zlnk.wait()
    set_links(1, plnk[...])

    def turn(ahead, behind):
        rows = []
        for ri in range(2):
            for r in range(3):
                for c in range(3):
                    j, k = ri * 9 + r * 3 + c, ri * 9 + c * 3 + r
                    back = -behind[k:k + 1] if ri == 0 else behind[k:k + 1]
                    rows.append(jnp.where(b == 0, ahead[j:j + 1], back))
        rows.append(jnp.zeros((64 - 18, sites), f32))
        return jnp.concatenate(rows, axis=0)

    set_links(2, turn(lnk[b, 0:18], plnk[0:18]))
    set_links(3, turn(plnk[0:18], zlnk[0:18]))

    got_pvec.wait()
    got_pedge = send(pvec.at[:, :, pl.ds(0, LZ), :], edge.at[1], mate)
    derive(2, 0, fetch_plain(theirs))
    contract(0, True)
    set_left(lambda ri, c: theirs(ri, c, everything))
    derive(1, 36, fetch_z(theirs))
    contract(2, False)
    got_pedge.wait()
    derive(1, 18, fetch_y(theirs, 1))
    contract(1, False)
    got_zvec.wait()
    derive(3, 0, fetch_plain(beyond))
    contract(0, False)
    for k in range(3):
        part[k * nv:(k + 1) * nv, :] = acc[k, :, :nv] + jnp.transpose(acc[k, :, nv:])

    offset = 0
    size = 3 * nv
    place = 0
    trail = []
    for m in [1] + zmasks:
        size //= 2
        bit = lax.rem(me // m, 2)
        kept = pl.multiple_of(offset + bit * size, 8)
        sent = pl.multiple_of(offset + (1 - bit) * size, 8)
        landing = pl.ds(place, size)
        copy = send(part.at[pl.ds(sent, size), :], recv.at[landing, :], flip(m))
        copy.wait()
        trail.append((m, kept, size))
        if m == ([1] + zmasks)[-1]:
            full[b, pl.ds(kept, size), :] = part[pl.ds(kept, size), :] + recv[landing, :]
        else:
            part[pl.ds(kept, size), :] += recv[landing, :]
        offset = kept
        place += size

    def share(t, at, rows, other):
        where = full.at[t, pl.ds(at, rows), :]
        return send(where, where, other)

    for m, kept, size in reversed(trail[1:]):
        share(b, kept, size, flip(m)).wait()
    _, kept, size = trail[0]
    over_y = share(b, kept, size, partner)
    over_core = share(b, kept, size, mate)
    over_core.wait()

    column = me * rl
    lane = pl.multiple_of((column // 128) * 128, 128)
    inside = column - lane

    def columns_of(t):
        for i in range(3):
            tcol[t, i] = jnp.transpose(full[t, i * nv:(i + 1) * nv, pl.ds(lane, 128)])

    columns_of(b)
    over_y.wait()
    share(1 - b, kept, size, mate).wait()
    columns_of(1 - b)

    def hot(condition):
        return jnp.where(condition, 1.0, 0.0).astype(f32)

    in_dir = [[hot(dirs[k] == i) for i in range(3)] for k in range(3)]
    in_group = [[hot(sgroup[t] == g) for t in range(2)] for g in range(NG)]
    my_group = [hot(bgroup[0] == g) for g in range(NG)]
    in_block = [sum(my_group[g] * in_group[g][t] for g in range(NG)) for t in range(2)]

    def rows_at(get, start):
        if rl % 8 == 0:
            return get(pl.ds(pl.multiple_of(start, 8), rl))
        base = pl.multiple_of((start // 8) * 8, 8)
        block = get(pl.ds(base, 8))
        rows = block[:rl]
        for j in range(1, 8 // rl):
            rows = jnp.where(start - base == j * rl, block[j * rl:(j + 1) * rl], rows)
        return rows

    plain = [
        [rows_at(lambda at: full[t, at, :], i * nv + column) for i in range(3)] for t in range(2)
    ]
    flipped = [[rows_at(lambda at: tcol[t, i, at, :], inside) for i in range(3)] for t in range(2)]
    for k in range(3):
        fwd = [sum(in_dir[k][i] * plain[t][i] for i in range(3)) for t in range(2)]
        bwd = [sum(in_dir[k][i] * flipped[t][i] for i in range(3)) for t in range(2)]
        for g in range(NG):
            one = in_group[g][0] * fwd[0] + in_group[g][1] * fwd[1]
            two = in_group[g][0] * bwd[0] + in_group[g][1] * bwd[1]
            elem[g, k, 0] = 0.25 * (one - two)
            elem[g, k, 1] = 0.25 * (one + two)

    total = jnp.zeros((nv, 4 * cb), f32)
    for k in range(3):
        chosen = jnp.zeros((nv, nv), f32)
        for t in range(2):
            for i in range(3):
                chosen += (in_block[t] * in_dir[k][i]) * full[t, i * nv:(i + 1) * nv, :]
        other = jnp.transpose(chosen)
        for ri, mat in enumerate((0.25 * (chosen - other), 0.25 * (chosen + other))):
            high, low = split(mat)
            rows = slice((2 * k + ri) * nv, (2 * k + ri + 1) * nv)
            total += jnp.dot(high, rhsh[rows, :], preferred_element_type=f32)
            total += jnp.dot(high, rhsl[rows, :], preferred_element_type=f32)
            total += jnp.dot(low, rhsh[rows, :], preferred_element_type=f32)

    zr = jnp.zeros((cb, cb), f32)
    zi = jnp.zeros((cb, cb), f32)
    for a in range(2):
        ur = jnp.transpose(per[0, a * nv:(a + 1) * nv, :])
        ui = jnp.transpose(per[1, a * nv:(a + 1) * nv, :])
        yr = total[:, a * cb:(a + 1) * cb]
        yi = total[:, (2 + a) * cb:(3 + a) * cb]
        dot = functools.partial(jnp.dot, precision=precise, preferred_element_type=f32)
        zr += dot(ur, yr) + dot(ui, yi)
        zi += dot(ur, yi) - dot(ui, yr)
    blocks[0] = zi - jnp.transpose(zi)
    blocks[1] = -(zr + jnp.transpose(zr))


def body(vectors, links, directions, slice_group, peram, block_group, *, n):
    nt, _, _, sites, nv = vectors.shape
    cb = peram.shape[2]
    lnk = jnp.pad(links.reshape(nt, 54, sites), ((0, 0), (0, 10), (0, 0)))
    vmem = pl.BlockSpec(memory_space=pltpu.VMEM)
    smem = pl.BlockSpec(memory_space=pltpu.SMEM)
    copies = 32
    return pl.pallas_call(
        functools.partial(kernel, n),
        out_shape=(
            jax.ShapeDtypeStruct((NG, 3, 2, nv // n, nv), f32),
            jax.ShapeDtypeStruct((2, cb, cb), f32),
        ),
        in_specs=[vmem, vmem, vmem, smem, smem, smem],
        out_specs=(vmem, vmem),
        scratch_shapes=[
            pltpu.VMEM((2, 3, sites, nv), f32),
            pltpu.VMEM((2, 3, sites, nv), f32),
            pltpu.VMEM((2, 2, 3, LZ, nv), f32),
            pltpu.VMEM((64, sites), f32),
            pltpu.VMEM((64, sites), f32),
            pltpu.VMEM((4, sites, 64), f32),
            pltpu.VMEM((nv, 6 * sites), bf16),
            pltpu.VMEM((nv, 6 * sites), bf16),
            pltpu.VMEM((6 * sites, 2 * nv), bf16),
            pltpu.VMEM((6 * sites, 2 * nv), bf16),
            pltpu.VMEM((3, nv, 2 * nv), f32),
            pltpu.VMEM((3 * nv, nv), f32),
            pltpu.VMEM((3 * nv, nv), f32),
            pltpu.VMEM((2, 3 * nv, nv), f32),
            pltpu.VMEM((2, 3, 128, nv), f32),
            pltpu.VMEM((6 * nv, 4 * cb), bf16),
            pltpu.VMEM((6 * nv, 4 * cb), bf16),
            pltpu.SemaphoreType.DMA((copies,)),
            pltpu.SemaphoreType.DMA((copies,)),
        ],
        compiler_params=pltpu.CompilerParams(
            collective_id=0, has_side_effects=True, vmem_limit_bytes=48 * 2**20
        ),
    )(vectors, lnk, peram, directions, slice_group, block_group)


def solution(mesh):
    return jax.shard_map(
        functools.partial(body, n=mesh.shape["space"]),
        mesh=mesh,
        in_specs=(
            P("cfg", None, None, "space", None),
            P("cfg", None, None, None, None, "space"),
            P(),
            P(),
            P("cfg", None, "space"),
            P("space"),
        ),
        out_specs=(P("cfg", None, None, "space", None), P("cfg", "space", None)),
        check_vma=False,
    )
```

```python
import functools

import jax
import jax.numpy as jnp
from jax import lax
from jax.experimental import pallas as pl
from jax.experimental.pallas import tpu as pltpu
from jax.sharding import PartitionSpec as P

NG = 2
LZ = 16
MESH = pl.DeviceIdType.MESH
f32 = jnp.float32
bf16 = jnp.bfloat16


def split(value):
    high = value.astype(bf16)
    return high, (value - high.astype(f32)).astype(bf16)


def kernel(
    n, vec, lnk, per, dirs, sgroup, bgroup, elem, blocks,
    pvec, zvec, edge, plnk, zlnk, ut, lth, ltl, xh, xl, acc, part, recv, full, tcol,
    perh, perl, pper, rows_out, rows_in, res_own, res_out, res_in, send_sem, recv_sem,
):
    sites = vec.shape[3]
    nv = vec.shape[4]
    cb = per.shape[1]
    rl = nv // n
    me = lax.axis_index("space")
    cfg = lax.axis_index("cfg")
    core = lax.rem(me, 2)
    b = lax.rem(me // 2, 2)

    def flip(mask):
        return me + mask * (1 - 2 * lax.rem(me // mask, 2))

    up = lax.rem(me + 4, n)
    down = lax.rem(me + n - 4, n)
    zmasks = []
    mask = 4
    while mask < n:
        zmasks.append(mask)
        mask *= 2
    others = [flip(1), flip(2), up, down] + [flip(m) for m in zmasks]
    barrier = pltpu.get_barrier_semaphore()
    for other in others:
        pl.semaphore_signal(barrier, inc=1, device_id=(cfg, other), device_id_type=MESH)
    pl.semaphore_wait(barrier, len(others))

    used = [0]

    def send(src, dst, other):
        i = used[0]
        used[0] += 1
        copy = pltpu.make_async_remote_copy(
            src_ref=src, dst_ref=dst, send_sem=send_sem.at[i], recv_sem=recv_sem.at[i],
            device_id=(cfg, other), device_id_type=MESH,
        )
        copy.start()
        return copy

    partner, mate = flip(2), flip(1)
    zdst = lax.rem(me + n + 8 * b - 4, n)
    got_edge = send(vec.at[b, :, :, pl.ds(0, LZ), :], edge.at[0], mate)
    got_plnk = send(lnk.at[1 - b], plnk, partner)
    got_zlnk = send(lnk.at[b], zlnk, zdst)
    got_pvec = send(vec.at[1 - b], pvec, partner)
    got_zvec = send(vec.at[b], zvec, zdst)

    def set_left(get):
        for ri in range(2):
            for c in range(3):
                j = ri * 3 + c
                high, low = split(jnp.transpose(get(ri, c)))
                lth[:, j * sites:(j + 1) * sites] = high
                ltl[:, j * sites:(j + 1) * sites] = low

    step = 16

    def derive(slot, column, fetch):
        def chunk(q, carry):
            base = pl.multiple_of(q * step, step)
            rows = pl.ds(base, step)
            link = ut[slot, rows, :]
            out_r = [None] * 3
            out_i = [None] * 3
            for c in range(3):
                vr = fetch(0, c, q, base)
                vi = fetch(1, c, q, base)
                for r in range(3):
                    j = column + r * 3 + c
                    lr = jnp.broadcast_to(link[:, j:j + 1], (step, nv))
                    li = jnp.broadcast_to(link[:, j + 9:j + 10], (step, nv))
                    tr = lr * vr - li * vi
                    ti = lr * vi + li * vr
                    out_r[r] = tr if c == 0 else out_r[r] + tr
                    out_i[r] = ti if c == 0 else out_i[r] + ti
            for r in range(3):
                plus = out_r[r] + out_i[r]
                minus = out_i[r] - out_r[r]
                ph, plo = split(plus)
                mh, mlo = split(minus)
                first = pl.ds(pl.multiple_of(r * sites + base, step), step)
                second = pl.ds(pl.multiple_of((3 + r) * sites + base, step), step)
                xh[first, :nv] = ph
                xl[first, :nv] = plo
                xh[second, :nv] = mh
                xl[second, :nv] = mlo
                xh[first, nv:] = mh
                xl[first, nv:] = mlo
                xh[second, nv:] = -ph
                xl[second, nv:] = -plo
            return carry

        lax.fori_loop(0, sites // step, chunk, 0)

    def contract(direction, first):
        prod = jnp.dot(lth[...], xh[...], preferred_element_type=f32)
        prod += jnp.dot(lth[...], xl[...], preferred_element_type=f32)
        prod += jnp.dot(ltl[...], xh[...], preferred_element_type=f32)
        if first:
            acc[direction] = prod
        else:
            acc[direction] += prod

    def set_links(slot, rows):
        ut[slot] = jnp.transpose(rows)

    def fetch_plain(get):
        return lambda ri, c, q, base: get(ri, c, pl.ds(base, step))

    def fetch_z(get):
        def fetch(ri, c, q, base):
            block = get(ri, c, pl.ds(base, step))
            return jnp.concatenate([block[1:], block[:1]], axis=0)
        return fetch

    def fetch_y(get, k):
        count = sites // LZ

        def fetch(ri, c, q, base):
            start = pl.multiple_of(lax.rem(q + 1, count) * step, step)
            inner = get(ri, c, pl.ds(start, step))
            return jnp.where(q == count - 1, edge[k, ri, c], inner)
        return fetch

    def own(ri, c, rows):
        return vec[b, ri, c, rows, :]

    def theirs(ri, c, rows):
        return pvec[ri, c, rows, :]

    def beyond(ri, c, rows):
        return zvec[ri, c, rows, :]

    everything = pl.ds(0, sites)
    set_left(lambda ri, c: own(ri, c, everything))
    set_links(0, lnk[b])
    derive(0, 36, fetch_z(own))
    contract(2, True)
    got_edge.wait()
    derive(0, 18, fetch_y(own, 0))
    contract(1, True)

    def set_peram(slot, source):
        lo = [[source[ri, :, (2 + s) * nv:(3 + s) * nv] for ri in range(2)] for s in range(2)]
        turned = [
            [lo[1], lo[0]],
            [[lo[1][1], -lo[1][0]], [-lo[0][1], lo[0][0]]],
            [lo[0], [-lo[1][0], -lo[1][1]]],
        ]
        rows = slice(slot * 4 * cb, (slot + 1) * 4 * cb)
        for k in range(3):
            (ar, ai), (br, bi) = turned[k]
            for part_of, stacked in enumerate(([ar, br, ai, bi], [-ai, -bi, ar, br])):
                high, low = split(jnp.concatenate(stacked, axis=0))
                lanes = slice((2 * k + part_of) * nv, (2 * k + part_of + 1) * nv)
                perh[rows, lanes] = high
                perl[rows, lanes] = low

    set_peram(0, per)

    got_plnk.wait()
    got_zlnk.wait()
    set_links(1, plnk[...])

    def turn(ahead, behind):
        rows = []
        for ri in range(2):
            for r in range(3):
                for c in range(3):
                    j, k = ri * 9 + r * 3 + c, ri * 9 + c * 3 + r
                    back = -behind[k:k + 1] if ri == 0 else behind[k:k + 1]
                    rows.append(jnp.where(b == 0, ahead[j:j + 1], back))
        rows.append(jnp.zeros((64 - 18, sites), f32))
        return jnp.concatenate(rows, axis=0)

    set_links(2, turn(lnk[b, 0:18], plnk[0:18]))
    set_links(3, turn(plnk[0:18], zlnk[0:18]))

    stages = [1] + zmasks

    def reduce_and_share(i):
        offset = 0
        size = nv
        place = 0
        trail = []
        for m in stages:
            size //= 2
            bit = lax.rem(me // m, 2)
            kept = pl.multiple_of(offset + bit * size, 8)
            sent = pl.multiple_of(offset + (1 - bit) * size, 8)
            landing = pl.ds(place, size)
            copy = send(part.at[i, pl.ds(sent, size), :], recv.at[i, landing, :], flip(m))
            yield
            copy.wait()
            trail.append((m, kept, size))
            total = part[i, pl.ds(kept, size), :] + recv[i, landing, :]
            if m == stages[-1]:
                full[i, pl.ds(kept, size), :] = total
            else:
                part[i, pl.ds(kept, size), :] = total
            offset = kept
            place += size
        for m, kept, size in reversed(trail):
            where = full.at[i, pl.ds(kept, size), :]
            copy = send(where, where, flip(m))
            yield
            copy.wait()

    def finish(k):
        part[k] = acc[k, :, :nv] + jnp.transpose(acc[k, :, nv:])

    got_pvec.wait()
    got_pedge = send(pvec.at[:, :, pl.ds(0, LZ), :], edge.at[1], mate)
    got_pper = send(per, pper, partner)
    derive(2, 0, fetch_plain(theirs))
    contract(0, True)
    set_left(lambda ri, c: theirs(ri, c, everything))
    derive(1, 36, fetch_z(theirs))
    contract(2, False)
    finish(2)
    moving_z = reduce_and_share(2)
    next(moving_z)
    got_pedge.wait()
    derive(1, 18, fetch_y(theirs, 1))
    next(moving_z)
    contract(1, False)
    finish(1)
    moving_y = reduce_and_share(1)
    next(moving_y)
    got_zvec.wait()
    derive(3, 0, fetch_plain(beyond))
    next(moving_z)
    next(moving_y)
    contract(0, False)
    finish(0)
    moving_x = reduce_and_share(0)
    moving = [moving_z, moving_y, moving_x]
    first = True
    while moving:
        moving = [one for one in moving if next(one, 0) is None]
        if first:
            first = False
            got_pper.wait()
            set_peram(1, pper)

    def hot(condition):
        return jnp.where(condition, 1.0, 0.0).astype(f32)

    in_dir = [[hot(dirs[k] == i) for i in range(3)] for k in range(3)]
    in_group = [[hot(sgroup[t] == g) for t in range(2)] for g in range(NG)]
    my_group = [hot(bgroup[0] == g) for g in range(NG)]
    in_block = [sum(my_group[g] * in_group[g][t] for g in range(NG)) for t in range(2)]

    lane = pl.multiple_of(((me * rl) // 128) * 128, 128)
    for i in range(3):
        tcol[i] = jnp.transpose(full[i, :, pl.ds(lane, 128)])

    def rows_at(get, start):
        if rl % 8 == 0:
            return get(pl.ds(pl.multiple_of(start, 8), rl))
        base = pl.multiple_of((start // 8) * 8, 8)
        block = get(pl.ds(base, 8))
        rows = block[:rl]
        for j in range(1, 8 // rl):
            rows = jnp.where(start - base == j * rl, block[j * rl:(j + 1) * rl], rows)
        return rows

    def rows_of(device, i):
        plain = rows_at(lambda at: full[i, at, :], device * rl)
        flipped = rows_at(lambda at: tcol[i, at, :], device * rl - lane)
        return 0.25 * (plain - flipped), 0.25 * (plain + flipped)

    for i in range(3):
        for ri, value in enumerate(rows_of(partner, i)):
            rows_out[i, ri, :rl] = value
    got_rows = send(rows_out, rows_in, partner)

    total = jnp.zeros((8 * cb, nv), f32)
    for k in range(3):
        chosen = sum(in_dir[k][i] * full[i] for i in range(3))
        other = jnp.transpose(chosen)
        for ri, mat in enumerate((0.25 * (other - chosen), 0.25 * (chosen + other))):
            high, low = split(mat)
            lanes = slice((2 * k + ri) * nv, (2 * k + ri + 1) * nv)
            total += jnp.dot(perh[:, lanes], high, preferred_element_type=f32)
            total += jnp.dot(perl[:, lanes], high, preferred_element_type=f32)
            total += jnp.dot(perh[:, lanes], low, preferred_element_type=f32)

    def against(left, right):
        return lax.dot_general(
            left, right, (((1,), (1,)), ((), ())), preferred_element_type=f32
        )

    def sided(slot, source, out):
        mine = total[slot * 4 * cb:(slot + 1) * 4 * cb]
        real = jnp.concatenate([mine[:cb], mine[cb:2 * cb]], axis=1)
        imag = jnp.concatenate([mine[2 * cb:3 * cb], mine[3 * cb:]], axis=1)
        yh, yl = split(jnp.concatenate([real, imag], axis=0))
        uh, ul = split(
            jnp.concatenate([source[0, :, :2 * nv], source[1, :, :2 * nv]], axis=0)
        )
        quads = against(uh, yh) + against(uh, yl) + against(ul, yh)
        zr = quads[:cb, :cb] + quads[cb:, cb:]
        zi = quads[:cb, cb:] - quads[cb:, :cb]
        out[0] = zi - jnp.transpose(zi)
        out[1] = -(zr + jnp.transpose(zr))

    sided(1, pper, res_out)
    got_res = send(res_out, res_in, partner)
    sided(0, per, res_own)

    mine = [rows_of(me, i) for i in range(3)]
    got_rows.wait()
    yours = [[rows_in[i, ri, :rl] for ri in range(2)] for i in range(3)]
    for k in range(3):
        for ri in range(2):
            here = sum(in_dir[k][i] * mine[i][ri] for i in range(3))
            there = sum(in_dir[k][i] * yours[i][ri] for i in range(3))
            by_time = [jnp.where(b == t, here, there) for t in range(2)]
            for g in range(NG):
                elem[g, k, ri] = in_group[g][0] * by_time[0] + in_group[g][1] * by_time[1]
    got_res.wait()
    weight = [jnp.where(b == 0, in_block[0], in_block[1]), jnp.where(b == 0, in_block[1], in_block[0])]
    blocks[...] = weight[0] * res_own[...] + weight[1] * res_in[...]


def body(vectors, links, directions, slice_group, peram, block_group, *, n):
    nt, _, _, sites, nv = vectors.shape
    cb = peram.shape[2]
    lnk = jnp.pad(links.reshape(nt, 54, sites), ((0, 0), (0, 10), (0, 0)))
    vmem = pl.BlockSpec(memory_space=pltpu.VMEM)
    smem = pl.BlockSpec(memory_space=pltpu.SMEM)
    copies = 64
    row_room = max(nv // n, 8)
    return pl.pallas_call(
        functools.partial(kernel, n),
        out_shape=(
            jax.ShapeDtypeStruct((NG, 3, 2, nv // n, nv), f32),
            jax.ShapeDtypeStruct((2, cb, cb), f32),
        ),
        in_specs=[vmem, vmem, vmem, smem, smem, smem],
        out_specs=(vmem, vmem),
        scratch_shapes=[
            pltpu.VMEM((2, 3, sites, nv), f32),
            pltpu.VMEM((2, 3, sites, nv), f32),
            pltpu.VMEM((2, 2, 3, LZ, nv), f32),
            pltpu.VMEM((64, sites), f32),
            pltpu.VMEM((64, sites), f32),
            pltpu.VMEM((4, sites, 64), f32),
            pltpu.VMEM((nv, 6 * sites), bf16),
            pltpu.VMEM((nv, 6 * sites), bf16),
            pltpu.VMEM((6 * sites, 2 * nv), bf16),
            pltpu.VMEM((6 * sites, 2 * nv), bf16),
            pltpu.VMEM((3, nv, 2 * nv), f32),
            pltpu.VMEM((3, nv, nv), f32),
            pltpu.VMEM((3, nv, nv), f32),
            pltpu.VMEM((3, nv, nv), f32),
            pltpu.VMEM((3, 128, nv), f32),
            pltpu.VMEM((8 * cb, 6 * nv), bf16),
            pltpu.VMEM((8 * cb, 6 * nv), bf16),
            pltpu.VMEM((2, cb, 4 * nv), f32),
            pltpu.VMEM((3, 2, row_room, nv), f32),
            pltpu.VMEM((3, 2, row_room, nv), f32),
            pltpu.VMEM((2, cb, cb), f32),
            pltpu.VMEM((2, cb, cb), f32),
            pltpu.VMEM((2, cb, cb), f32),
            pltpu.SemaphoreType.DMA((copies,)),
            pltpu.SemaphoreType.DMA((copies,)),
        ],
        compiler_params=pltpu.CompilerParams(
            collective_id=0, has_side_effects=True, vmem_limit_bytes=48 * 2**20
        ),
    )(vectors, lnk, jnp.swapaxes(peram, 1, 2), directions, slice_group, block_group)


def solution(mesh):
    return jax.shard_map(
        functools.partial(body, n=mesh.shape["space"]),
        mesh=mesh,
        in_specs=(
            P("cfg", None, None, "space", None),
            P("cfg", None, None, None, None, "space"),
            P(),
            P(),
            P("cfg", None, "space"),
            P("space"),
        ),
        out_specs=(P("cfg", None, None, "space", None), P("cfg", "space", None)),
        check_vma=False,
    )
```

```python
import functools

import jax
import jax.numpy as jnp
from jax import lax
from jax.experimental import pallas as pl
from jax.experimental.pallas import tpu as pltpu
from jax.sharding import PartitionSpec as P

NG = 2
LZ = 16
CHUNKS = 4
MESH = pl.DeviceIdType.MESH
f32 = jnp.float32
bf16 = jnp.bfloat16


def split(value):
    high = value.astype(bf16)
    return high, (value - high.astype(f32)).astype(bf16)


def kernel(
    n, vec, lnk, per_hbm, dirs, sgroup, bgroup, elem, blocks,
    ovec, olnk, per, pvec, zvec, edge, plnk, zlnk, ut, lth, ltl, xh, xl, acc, part, recv, full, tcol,
    perh, perl, pper, rows_out, rows_in, res_own, res_out, res_in, send_sem, recv_sem,
    vec_send, vec_recv, edge_send, edge_recv, local_sem,
):
    sites = vec.shape[3]
    nv = vec.shape[4]
    cb = per_hbm.shape[1]
    rl = nv // n
    me = lax.axis_index("space")
    cfg = lax.axis_index("cfg")
    core = lax.rem(me, 2)
    b = lax.rem(me // 2, 2)

    def flip(mask):
        return me + mask * (1 - 2 * lax.rem(me // mask, 2))

    up = lax.rem(me + 4, n)
    down = lax.rem(me + n - 4, n)
    zmasks = []
    mask = 4
    while mask < n:
        zmasks.append(mask)
        mask *= 2
    others = [flip(1), flip(2), up, down] + [flip(m) for m in zmasks]
    local = [
        pltpu.make_async_copy(src, dst, local_sem.at[k])
        for k, (src, dst) in enumerate(((vec.at[b], ovec), (lnk.at[b], olnk), (per_hbm, per)))
    ]
    for copy in local:
        copy.start()
    barrier = pltpu.get_barrier_semaphore()
    for other in others:
        pl.semaphore_signal(barrier, inc=1, device_id=(cfg, other), device_id_type=MESH)
    pl.semaphore_wait(barrier, len(others))

    used = [0]

    def send(src, dst, other):
        i = used[0]
        used[0] += 1
        copy = pltpu.make_async_remote_copy(
            src_ref=src, dst_ref=dst, send_sem=send_sem.at[i], recv_sem=recv_sem.at[i],
            device_id=(cfg, other), device_id_type=MESH,
        )
        copy.start()
        return copy

    partner, mate = flip(2), flip(1)
    zdst = lax.rem(me + n + 8 * b - 4, n)
    width = sites // CHUNKS

    def piece(h):
        return pl.ds(pl.multiple_of(h * width, width), width)

    def vec_copies(h):
        return [
            pltpu.make_async_remote_copy(
                src_ref=vec.at[t, :, :, piece(h), :], dst_ref=dst.at[:, :, piece(h), :],
                send_sem=vec_send.at[k, h], recv_sem=vec_recv.at[k, h],
                device_id=(cfg, other), device_id_type=MESH,
            )
            for k, (t, dst, other) in enumerate(((1 - b, pvec, partner), (b, zvec, zdst)))
        ]

    def start_vec(h):
        for copy in vec_copies(h):
            copy.start()

    got_plnk = send(lnk.at[1 - b], plnk, partner)
    got_zlnk = send(lnk.at[b], zlnk, zdst)
    start_vec(0)
    got_edge = send(vec.at[b, :, :, pl.ds(0, LZ), :], edge.at[0], mate)
    start_vec(1)
    for copy in local:
        copy.wait()

    def set_left(slot, h, source):
        rows = [source[ri, c, piece(h), :] for ri in range(2) for c in range(3)]
        high, low = split(jnp.transpose(jnp.concatenate(rows, axis=0)))
        lth[slot, h] = high
        ltl[slot, h] = low

    step = 16

    def derive(buf, h, slot, fetch):
        for q in range(width // step):
            base = pl.multiple_of(h * width + q * step, step)
            link = ut[slot, pl.ds(base, step), :]
            out_r = [None] * 3
            out_i = [None] * 3
            for c in range(3):
                vr = fetch(0, c, base)
                vi = fetch(1, c, base)
                for r in range(3):
                    j = (r * 3 + c) * 2
                    lr = jnp.broadcast_to(link[:, j:j + 1], (step, nv))
                    li = jnp.broadcast_to(link[:, j + 1:j + 2], (step, nv))
                    tr = lr * vr - li * vi
                    ti = lr * vi + li * vr
                    out_r[r] = tr if c == 0 else out_r[r] + tr
                    out_i[r] = ti if c == 0 else out_i[r] + ti
            for r in range(3):
                plus = out_r[r] + out_i[r]
                minus = out_i[r] - out_r[r]
                ph, plo = split(plus)
                mh, mlo = split(minus)
                first = slice(r * width + q * step, r * width + (q + 1) * step)
                second = slice((3 + r) * width + q * step, (3 + r) * width + (q + 1) * step)
                xh[buf, first, :nv] = ph
                xl[buf, first, :nv] = plo
                xh[buf, second, :nv] = mh
                xl[buf, second, :nv] = mlo
                xh[buf, first, nv:] = mh
                xl[buf, first, nv:] = mlo
                xh[buf, second, nv:] = -ph
                xl[buf, second, nv:] = -plo

    def unit(buf, direction, left, h, slot, fetch):
        derive(buf, h, slot, fetch)
        prod = jnp.dot(lth[left, h], xh[buf], preferred_element_type=f32)
        prod += jnp.dot(lth[left, h], xl[buf], preferred_element_type=f32)
        prod += jnp.dot(ltl[left, h], xh[buf], preferred_element_type=f32)
        acc[direction] += prod

    def fetch_plain(source):
        return lambda ri, c, base: source[ri, c, pl.ds(base, step), :]

    def fetch_z(source):
        def fetch(ri, c, base):
            block = source[ri, c, pl.ds(base, step), :]
            return jnp.concatenate([block[1:], block[:1]], axis=0)
        return fetch

    def fetch_y(source, k):
        def fetch(ri, c, base):
            start = pl.multiple_of(lax.rem(base + step, sites), step)
            inner = source[ri, c, pl.ds(start, step), :]
            return jnp.where(base == sites - step, edge[k, ri, c], inner)
        return fetch

    def fetch_next(source):
        return lambda ri, c, base: source[ri, c, pl.ds(base + step, step), :]

    def rows_of_link(get):
        return [get(r, c) for r in range(3) for c in range(3)]

    def set_links(slot, pairs):
        pairs = pairs + [jnp.zeros((64 - 18, sites), f32)]
        ut[slot] = jnp.transpose(jnp.concatenate(pairs, axis=0))

    for k in range(3):
        acc[k] = jnp.zeros((nv, 2 * nv), f32)
    set_links(0, rows_of_link(lambda r, c: olnk[2, r, c]))
    set_links(1, rows_of_link(lambda r, c: olnk[1, r, c]))
    got_edge.wait()

    def own_chunk(h, carry):
        set_left(0, h, ovec)
        unit(0, 2, 0, h, 0, fetch_z(ovec))
        unit(1, 1, 0, h, 1, fetch_y(ovec, 0))
        return carry

    lax.fori_loop(0, CHUNKS, own_chunk, 0)

    def set_peram(slot, source):
        lo = [[source[ri, :, (2 + s) * nv:(3 + s) * nv] for ri in range(2)] for s in range(2)]
        turned = [
            [lo[1], lo[0]],
            [[lo[1][1], -lo[1][0]], [-lo[0][1], lo[0][0]]],
            [lo[0], [-lo[1][0], -lo[1][1]]],
        ]
        rows = slice(slot * 4 * cb, (slot + 1) * 4 * cb)
        for k in range(3):
            (ar, ai), (br, bi) = turned[k]
            for part_of, stacked in enumerate(([ar, br, ai, bi], [-ai, -bi, ar, br])):
                high, low = split(jnp.concatenate(stacked, axis=0))
                lanes = slice((2 * k + part_of) * nv, (2 * k + part_of + 1) * nv)
                perh[rows, lanes] = high
                perl[rows, lanes] = low

    set_peram(0, per)

    got_plnk.wait()
    got_zlnk.wait()
    set_links(2, rows_of_link(lambda r, c: plnk[2, r, c]))
    set_links(3, rows_of_link(lambda r, c: plnk[1, r, c]))
    sign = jnp.where(lax.broadcasted_iota(jnp.int32, (2, sites), 0) == 0, -1.0, 1.0)

    def turn(ahead, behind):
        return rows_of_link(
            lambda r, c: jnp.where(b == 0, ahead[0, r, c], sign * behind[0, c, r])
        )

    set_links(4, turn(olnk, plnk))
    set_links(5, turn(plnk, zlnk))

    stages = [1] + zmasks

    def reduce_and_share(i):
        offset = 0
        size = nv
        place = 0
        trail = []
        for m in stages:
            size //= 2
            bit = lax.rem(me // m, 2)
            kept = pl.multiple_of(offset + bit * size, 8)
            sent = pl.multiple_of(offset + (1 - bit) * size, 8)
            landing = pl.ds(place, size)
            copy = send(part.at[i, pl.ds(sent, size), :], recv.at[i, landing, :], flip(m))
            yield
            copy.wait()
            trail.append((m, kept, size))
            total = part[i, pl.ds(kept, size), :] + recv[i, landing, :]
            if m == stages[-1]:
                full[i, pl.ds(kept, size), :] = total
            else:
                part[i, pl.ds(kept, size), :] = total
            offset = kept
            place += size
        for m, kept, size in reversed(trail):
            where = full.at[i, pl.ds(kept, size), :]
            copy = send(where, where, flip(m))
            yield
            copy.wait()

    def finish(k):
        part[k] = acc[k, :, :nv] + jnp.transpose(acc[k, :, nv:])

    def edge_copy():
        return pltpu.make_async_remote_copy(
            src_ref=pvec.at[:, :, pl.ds(0, LZ), :], dst_ref=edge.at[1],
            send_sem=edge_send, recv_sem=edge_recv,
            device_id=(cfg, mate), device_id_type=MESH,
        )

    def chunk_x(h):
        unit(0, 0, 0, h, 4, fetch_plain(pvec))
        unit(1, 0, 1, h, 5, fetch_plain(zvec))

    def chunk_z(h):
        set_left(1, h, pvec)
        unit(0, 2, 1, h, 2, fetch_z(pvec))

    def arrived(h):
        for copy in vec_copies(h):
            copy.wait()

    def their_chunk(h, carry):
        arrived(h)
        if CHUNKS > 2:
            pl.when(h + 2 < CHUNKS)(lambda: start_vec(h + 2))
        pl.when(h == 0)(lambda: edge_copy().start())
        chunk_z(h)
        chunk_x(h)
        pl.when(h > 0)(lambda: unit(0, 1, 1, h - 1, 3, fetch_next(pvec)))
        return carry

    last = CHUNKS - 1
    lax.fori_loop(0, last, their_chunk, 0)
    arrived(last)
    got_pper = send(per, pper, partner)
    chunk_z(last)
    finish(2)
    moving_z = reduce_and_share(2)
    next(moving_z)
    edge_copy().wait()
    unit(1, 1, 1, last - 1, 3, fetch_next(pvec))
    unit(0, 1, 1, last, 3, fetch_y(pvec, 1))
    finish(1)
    next(moving_z)
    moving_y = reduce_and_share(1)
    next(moving_y)
    chunk_x(last)
    finish(0)
    moving_x = reduce_and_share(0)
    moving = [moving_z, moving_y, moving_x]
    first = True
    while moving:
        moving = [one for one in moving if next(one, 0) is None]
        if first:
            first = False
            got_pper.wait()
            set_peram(1, pper)

    def hot(condition):
        return jnp.where(condition, 1.0, 0.0).astype(f32)

    in_dir = [[hot(dirs[k] == i) for i in range(3)] for k in range(3)]
    in_group = [[hot(sgroup[t] == g) for t in range(2)] for g in range(NG)]
    my_group = [hot(bgroup[0] == g) for g in range(NG)]
    in_block = [sum(my_group[g] * in_group[g][t] for g in range(NG)) for t in range(2)]

    lane = pl.multiple_of(((me * rl) // 128) * 128, 128)
    for i in range(3):
        tcol[i] = jnp.transpose(full[i, :, pl.ds(lane, 128)])

    def rows_at(get, start):
        if rl % 8 == 0:
            return get(pl.ds(pl.multiple_of(start, 8), rl))
        base = pl.multiple_of((start // 8) * 8, 8)
        block = get(pl.ds(base, 8))
        rows = block[:rl]
        for j in range(1, 8 // rl):
            rows = jnp.where(start - base == j * rl, block[j * rl:(j + 1) * rl], rows)
        return rows

    def rows_of(device, i):
        plain = rows_at(lambda at: full[i, at, :], device * rl)
        flipped = rows_at(lambda at: tcol[i, at, :], device * rl - lane)
        return 0.25 * (plain - flipped), 0.25 * (plain + flipped)

    for i in range(3):
        for ri, value in enumerate(rows_of(partner, i)):
            rows_out[i, ri, :rl] = value
    got_rows = send(rows_out, rows_in, partner)

    total = jnp.zeros((8 * cb, nv), f32)
    for k in range(3):
        chosen = sum(in_dir[k][i] * full[i] for i in range(3))
        other = jnp.transpose(chosen)
        for ri, mat in enumerate((0.25 * (other - chosen), 0.25 * (chosen + other))):
            high, low = split(mat)
            lanes = slice((2 * k + ri) * nv, (2 * k + ri + 1) * nv)
            total += jnp.dot(perh[:, lanes], high, preferred_element_type=f32)
            total += jnp.dot(perl[:, lanes], high, preferred_element_type=f32)
            total += jnp.dot(perh[:, lanes], low, preferred_element_type=f32)

    def against(left, right):
        return lax.dot_general(
            left, right, (((1,), (1,)), ((), ())), preferred_element_type=f32
        )

    def sided(slot, source, out):
        mine = total[slot * 4 * cb:(slot + 1) * 4 * cb]
        real = jnp.concatenate([mine[:cb], mine[cb:2 * cb]], axis=1)
        imag = jnp.concatenate([mine[2 * cb:3 * cb], mine[3 * cb:]], axis=1)
        yh, yl = split(jnp.concatenate([real, imag], axis=0))
        uh, ul = split(
            jnp.concatenate([source[0, :, :2 * nv], source[1, :, :2 * nv]], axis=0)
        )
        quads = against(uh, yh) + against(uh, yl) + against(ul, yh)
        zr = quads[:cb, :cb] + quads[cb:, cb:]
        zi = quads[:cb, cb:] - quads[cb:, :cb]
        out[0] = zi - jnp.transpose(zi)
        out[1] = -(zr + jnp.transpose(zr))

    sided(1, pper, res_out)
    got_res = send(res_out, res_in, partner)
    sided(0, per, res_own)

    mine = [rows_of(me, i) for i in range(3)]
    got_rows.wait()
    yours = [[rows_in[i, ri, :rl] for ri in range(2)] for i in range(3)]
    for k in range(3):
        for ri in range(2):
            here = sum(in_dir[k][i] * mine[i][ri] for i in range(3))
            there = sum(in_dir[k][i] * yours[i][ri] for i in range(3))
            by_time = [jnp.where(b == t, here, there) for t in range(2)]
            for g in range(NG):
                elem[g, k, ri] = in_group[g][0] * by_time[0] + in_group[g][1] * by_time[1]
    got_res.wait()
    weight = [jnp.where(b == 0, in_block[0], in_block[1]), jnp.where(b == 0, in_block[1], in_block[0])]
    blocks[...] = weight[0] * res_own[...] + weight[1] * res_in[...]


def body(vectors, links, directions, slice_group, peram, block_group, *, n):
    nt, _, _, sites, nv = vectors.shape
    cb = peram.shape[2]
    lnk = jnp.transpose(links, (0, 1, 3, 4, 2, 5))
    hbm = pl.BlockSpec(memory_space=pltpu.HBM)
    vmem = pl.BlockSpec(memory_space=pltpu.VMEM)
    smem = pl.BlockSpec(memory_space=pltpu.SMEM)
    copies = 64
    row_room = max(nv // n, 8)
    return pl.pallas_call(
        functools.partial(kernel, n),
        out_shape=(
            jax.ShapeDtypeStruct((NG, 3, 2, nv // n, nv), f32),
            jax.ShapeDtypeStruct((2, cb, cb), f32),
        ),
        in_specs=[hbm, hbm, hbm, smem, smem, smem],
        out_specs=(vmem, vmem),
        scratch_shapes=[
            pltpu.VMEM((2, 3, sites, nv), f32),
            pltpu.VMEM((3, 3, 3, 2, sites), f32),
            pltpu.VMEM((2, cb, 4 * nv), f32),
            pltpu.VMEM((2, 3, sites, nv), f32),
            pltpu.VMEM((2, 3, sites, nv), f32),
            pltpu.VMEM((2, 2, 3, LZ, nv), f32),
            pltpu.VMEM((3, 3, 3, 2, sites), f32),
            pltpu.VMEM((3, 3, 3, 2, sites), f32),
            pltpu.VMEM((6, sites, 64), f32),
            pltpu.VMEM((2, CHUNKS, nv, 6 * sites // CHUNKS), bf16),
            pltpu.VMEM((2, CHUNKS, nv, 6 * sites // CHUNKS), bf16),
            pltpu.VMEM((2, 6 * sites // CHUNKS, 2 * nv), bf16),
            pltpu.VMEM((2, 6 * sites // CHUNKS, 2 * nv), bf16),
            pltpu.VMEM((3, nv, 2 * nv), f32),
            pltpu.VMEM((3, nv, nv), f32),
            pltpu.VMEM((3, nv, nv), f32),
            pltpu.VMEM((3, nv, nv), f32),
            pltpu.VMEM((3, 128, nv), f32),
            pltpu.VMEM((8 * cb, 6 * nv), bf16),
            pltpu.VMEM((8 * cb, 6 * nv), bf16),
            pltpu.VMEM((2, cb, 4 * nv), f32),
            pltpu.VMEM((3, 2, row_room, nv), f32),
            pltpu.VMEM((3, 2, row_room, nv), f32),
            pltpu.VMEM((2, cb, cb), f32),
            pltpu.VMEM((2, cb, cb), f32),
            pltpu.VMEM((2, cb, cb), f32),
            pltpu.SemaphoreType.DMA((copies,)),
            pltpu.SemaphoreType.DMA((copies,)),
            pltpu.SemaphoreType.DMA((2, CHUNKS)),
            pltpu.SemaphoreType.DMA((2, CHUNKS)),
            pltpu.SemaphoreType.DMA,
            pltpu.SemaphoreType.DMA,
            pltpu.SemaphoreType.DMA((3,)),
        ],
        compiler_params=pltpu.CompilerParams(
            collective_id=0, has_side_effects=True, vmem_limit_bytes=48 * 2**20
        ),
    )(vectors, lnk, jnp.swapaxes(peram, 1, 2), directions, slice_group, block_group)


def solution(mesh):
    return jax.shard_map(
        functools.partial(body, n=mesh.shape["space"]),
        mesh=mesh,
        in_specs=(
            P("cfg", None, None, "space", None),
            P("cfg", None, None, None, None, "space"),
            P(),
            P(),
            P("cfg", None, "space"),
            P("space"),
        ),
        out_specs=(P("cfg", None, None, "space", None), P("cfg", "space", None)),
        check_vma=False,
    )
```

```python
import functools

import jax
import jax.numpy as jnp
from jax import lax
from jax.experimental import pallas as pl
from jax.experimental.pallas import tpu as pltpu
from jax.sharding import PartitionSpec as P

NG = 2
LZ = 16
CHUNKS = 4
MESH = pl.DeviceIdType.MESH
f32 = jnp.float32
bf16 = jnp.bfloat16


def split(value):
    high = value.astype(bf16)
    return high, (value - high.astype(f32)).astype(bf16)


def kernel(
    n, vec, lnk, per_hbm, dirs, sgroup, bgroup, elem, blocks,
    ovec, olnk, per, pvec, zvec, edge, plnk, zlnk, ut, lth, ltl, xh, xl, acc, part, recv, full, tcol,
    perh, perl, pper, rows_out, rows_in, res_own, res_out, res_in, send_sem, recv_sem,
    vec_send, vec_recv, edge_send, edge_recv, local_sem,
):
    sites = vec.shape[3]
    nv = vec.shape[4]
    cb = per_hbm.shape[1]
    rl = nv // n
    me = lax.axis_index("space")
    cfg = lax.axis_index("cfg")
    core = lax.rem(me, 2)
    b = lax.rem(me // 2, 2)

    def flip(mask):
        return me + mask * (1 - 2 * lax.rem(me // mask, 2))

    up = lax.rem(me + 4, n)
    down = lax.rem(me + n - 4, n)
    zmasks = []
    mask = 4
    while mask < n:
        zmasks.append(mask)
        mask *= 2
    others = [flip(1), flip(2), up, down] + [flip(m) for m in zmasks]
    local = [
        pltpu.make_async_copy(src, dst, local_sem.at[k])
        for k, (src, dst) in enumerate(((vec.at[b], ovec), (lnk.at[b], olnk), (per_hbm, per)))
    ]
    for copy in local:
        copy.start()
    barrier = pltpu.get_barrier_semaphore()
    for other in others:
        pl.semaphore_signal(barrier, inc=1, device_id=(cfg, other), device_id_type=MESH)
    pl.semaphore_wait(barrier, len(others))

    used = [0]

    def send(src, dst, other):
        i = used[0]
        used[0] += 1
        copy = pltpu.make_async_remote_copy(
            src_ref=src, dst_ref=dst, send_sem=send_sem.at[i], recv_sem=recv_sem.at[i],
            device_id=(cfg, other), device_id_type=MESH,
        )
        copy.start()
        return copy

    partner, mate = flip(2), flip(1)
    zdst = lax.rem(me + n + 8 * b - 4, n)
    width = sites // CHUNKS

    def piece(h):
        return pl.ds(pl.multiple_of(h * width, width), width)

    def vec_copies(h):
        return [
            pltpu.make_async_remote_copy(
                src_ref=vec.at[t, :, :, piece(h), :], dst_ref=dst.at[:, :, piece(h), :],
                send_sem=vec_send.at[k, h], recv_sem=vec_recv.at[k, h],
                device_id=(cfg, other), device_id_type=MESH,
            )
            for k, (t, dst, other) in enumerate(((1 - b, pvec, partner), (b, zvec, zdst)))
        ]

    def start_vec(h):
        for copy in vec_copies(h):
            copy.start()

    got_plnk = send(lnk.at[1 - b], plnk, partner)
    got_zlnk = send(lnk.at[b], zlnk, zdst)
    start_vec(0)
    got_edge = send(vec.at[b, :, :, pl.ds(0, LZ), :], edge.at[0], mate)
    start_vec(1)
    for copy in local:
        copy.wait()

    def set_left(slot, h, source):
        rows = [source[ri, c, piece(h), :] for ri in range(2) for c in range(3)]
        high, low = split(jnp.transpose(jnp.concatenate(rows, axis=0)))
        lth[slot, h] = high
        ltl[slot, h] = low

    step = 16

    def derive(buf, h, slot, fetch):
        for q in range(width // step):
            base = pl.multiple_of(h * width + q * step, step)
            link = ut[slot, pl.ds(base, step), :]
            out_r = [None] * 3
            out_i = [None] * 3
            for c in range(3):
                vr = fetch(0, c, base)
                vi = fetch(1, c, base)
                for r in range(3):
                    j = (r * 3 + c) * 2
                    lr = jnp.broadcast_to(link[:, j:j + 1], (step, nv))
                    li = jnp.broadcast_to(link[:, j + 1:j + 2], (step, nv))
                    tr = lr * vr - li * vi
                    ti = lr * vi + li * vr
                    out_r[r] = tr if c == 0 else out_r[r] + tr
                    out_i[r] = ti if c == 0 else out_i[r] + ti
            for r in range(3):
                plus = out_r[r] + out_i[r]
                minus = out_i[r] - out_r[r]
                ph, plo = split(plus)
                mh, mlo = split(minus)
                first = slice(r * width + q * step, r * width + (q + 1) * step)
                second = slice((3 + r) * width + q * step, (3 + r) * width + (q + 1) * step)
                xh[buf, first, :nv] = ph
                xl[buf, first, :nv] = plo
                xh[buf, second, :nv] = mh
                xl[buf, second, :nv] = mlo
                xh[buf, first, nv:] = mh
                xl[buf, first, nv:] = mlo
                xh[buf, second, nv:] = -ph
                xl[buf, second, nv:] = -plo

    def unit(buf, direction, left, h, slot, fetch):
        derive(buf, h, slot, fetch)
        prod = jnp.dot(lth[left, h], xh[buf], preferred_element_type=f32)
        prod += jnp.dot(lth[left, h], xl[buf], preferred_element_type=f32)
        prod += jnp.dot(ltl[left, h], xh[buf], preferred_element_type=f32)
        acc[direction] += prod

    def fetch_plain(source):
        return lambda ri, c, base: source[ri, c, pl.ds(base, step), :]

    def fetch_z(source):
        def fetch(ri, c, base):
            block = source[ri, c, pl.ds(base, step), :]
            return jnp.concatenate([block[1:], block[:1]], axis=0)
        return fetch

    def fetch_y(source, k):
        def fetch(ri, c, base):
            start = pl.multiple_of(lax.rem(base + step, sites), step)
            inner = source[ri, c, pl.ds(start, step), :]
            return jnp.where(base == sites - step, edge[k, ri, c], inner)
        return fetch

    def fetch_next(source):
        return lambda ri, c, base: source[ri, c, pl.ds(base + step, step), :]

    def rows_of_link(get):
        return [get(r, c) for r in range(3) for c in range(3)]

    def set_links(slot, pairs):
        pairs = pairs + [jnp.zeros((64 - 18, sites), f32)]
        ut[slot] = jnp.transpose(jnp.concatenate(pairs, axis=0))

    for k in range(3):
        acc[k] = jnp.zeros((nv, 2 * nv), f32)
    set_links(0, rows_of_link(lambda r, c: olnk[2, r, c]))
    set_links(1, rows_of_link(lambda r, c: olnk[1, r, c]))
    got_edge.wait()

    def own_chunk(h, carry):
        set_left(0, h, ovec)
        unit(0, 2, 0, h, 0, fetch_z(ovec))
        unit(1, 1, 0, h, 1, fetch_y(ovec, 0))
        return carry

    lax.fori_loop(0, CHUNKS, own_chunk, 0)

    def set_peram(slot, source):
        lo = [[source[ri, :, (2 + s) * nv:(3 + s) * nv] for ri in range(2)] for s in range(2)]
        turned = [
            [lo[1], lo[0]],
            [[lo[1][1], -lo[1][0]], [-lo[0][1], lo[0][0]]],
            [lo[0], [-lo[1][0], -lo[1][1]]],
        ]
        rows = slice(slot * 4 * cb, (slot + 1) * 4 * cb)
        for k in range(3):
            (ar, ai), (br, bi) = turned[k]
            for part_of, stacked in enumerate(([ar, br, ai, bi], [-ai, -bi, ar, br])):
                high, low = split(jnp.concatenate(stacked, axis=0))
                lanes = slice((2 * k + part_of) * nv, (2 * k + part_of + 1) * nv)
                perh[rows, lanes] = high
                perl[rows, lanes] = low

    set_peram(0, per)

    got_plnk.wait()
    got_zlnk.wait()
    set_links(2, rows_of_link(lambda r, c: plnk[2, r, c]))
    set_links(3, rows_of_link(lambda r, c: plnk[1, r, c]))
    sign = jnp.where(lax.broadcasted_iota(jnp.int32, (2, sites), 0) == 0, -1.0, 1.0)

    def turn(ahead, behind):
        return rows_of_link(
            lambda r, c: jnp.where(b == 0, ahead[0, r, c], sign * behind[0, c, r])
        )

    set_links(4, turn(olnk, plnk))
    set_links(5, turn(plnk, zlnk))

    stages = [1] + zmasks

    def reduce_and_share(i):
        offset = 0
        size = nv
        place = 0
        trail = []
        for m in stages:
            size //= 2
            bit = lax.rem(me // m, 2)
            kept = pl.multiple_of(offset + bit * size, 8)
            sent = pl.multiple_of(offset + (1 - bit) * size, 8)
            landing = pl.ds(place, size)
            copy = send(part.at[i, pl.ds(sent, size), :], recv.at[i, landing, :], flip(m))
            yield
            copy.wait()
            trail.append((m, kept, size))
            total = part[i, pl.ds(kept, size), :] + recv[i, landing, :]
            if m == stages[-1]:
                full[i, pl.ds(kept, size), :] = total
            else:
                part[i, pl.ds(kept, size), :] = total
            offset = kept
            place += size
        for m, kept, size in reversed(trail):
            where = full.at[i, pl.ds(kept, size), :]
            copy = send(where, where, flip(m))
            yield
            copy.wait()

    def finish(k):
        part[k] = acc[k, :, :nv] + jnp.transpose(acc[k, :, nv:])

    def edge_copy():
        return pltpu.make_async_remote_copy(
            src_ref=pvec.at[:, :, pl.ds(0, LZ), :], dst_ref=edge.at[1],
            send_sem=edge_send, recv_sem=edge_recv,
            device_id=(cfg, mate), device_id_type=MESH,
        )

    def chunk_x(h):
        unit(0, 0, 0, h, 4, fetch_plain(pvec))
        unit(1, 0, 1, h, 5, fetch_plain(zvec))

    def chunk_z(h):
        set_left(1, h, pvec)
        unit(0, 2, 1, h, 2, fetch_z(pvec))

    def arrived(h):
        for copy in vec_copies(h):
            copy.wait()

    def their_chunk(h, carry):
        arrived(h)
        if CHUNKS > 2:
            pl.when(h + 2 < CHUNKS)(lambda: start_vec(h + 2))
        pl.when(h == 0)(lambda: edge_copy().start())
        chunk_z(h)
        chunk_x(h)
        pl.when(h > 0)(lambda: unit(0, 1, 1, h - 1, 3, fetch_next(pvec)))
        return carry

    last = CHUNKS - 1
    lax.fori_loop(0, last, their_chunk, 0)
    arrived(last)
    got_pper = send(per, pper, partner)
    chunk_z(last)
    finish(2)
    moving_z = reduce_and_share(2)
    next(moving_z)
    edge_copy().wait()
    unit(1, 1, 1, last - 1, 3, fetch_next(pvec))
    unit(0, 1, 1, last, 3, fetch_y(pvec, 1))
    finish(1)
    next(moving_z)
    moving_y = reduce_and_share(1)
    next(moving_y)
    chunk_x(last)
    finish(0)
    moving_x = reduce_and_share(0)
    moving = [moving_z, moving_y, moving_x]
    first = True
    while moving:
        moving = [one for one in moving if next(one, 0) is None]
        if first:
            first = False
            got_pper.wait()
            set_peram(1, pper)

    def hot(condition):
        return jnp.where(condition, 1.0, 0.0).astype(f32)

    in_dir = [[hot(dirs[k] == i) for i in range(3)] for k in range(3)]
    in_group = [[hot(sgroup[t] == g) for t in range(2)] for g in range(NG)]
    my_group = [hot(bgroup[0] == g) for g in range(NG)]
    in_block = [sum(my_group[g] * in_group[g][t] for g in range(NG)) for t in range(2)]

    lane = pl.multiple_of(((me * rl) // 128) * 128, 128)
    for i in range(3):
        tcol[i] = jnp.transpose(full[i, :, pl.ds(lane, 128)])

    def rows_at(get, start):
        if rl % 8 == 0:
            return get(pl.ds(pl.multiple_of(start, 8), rl))
        base = pl.multiple_of((start // 8) * 8, 8)
        block = get(pl.ds(base, 8))
        rows = block[:rl]
        for j in range(1, 8 // rl):
            rows = jnp.where(start - base == j * rl, block[j * rl:(j + 1) * rl], rows)
        return rows

    def rows_of(device, i):
        plain = rows_at(lambda at: full[i, at, :], device * rl)
        flipped = rows_at(lambda at: tcol[i, at, :], device * rl - lane)
        return 0.25 * (plain - flipped), 0.25 * (plain + flipped)

    for i in range(3):
        for ri, value in enumerate(rows_of(partner, i)):
            rows_out[i, ri, :rl] = value
    got_rows = send(rows_out, rows_in, partner)

    total = jnp.zeros((8 * cb, nv), f32)
    for k in range(3):
        chosen = sum(in_dir[k][i] * full[i] for i in range(3))
        other = jnp.transpose(chosen)
        for ri, mat in enumerate((0.25 * (other - chosen), 0.25 * (chosen + other))):
            high, low = split(mat)
            lanes = slice((2 * k + ri) * nv, (2 * k + ri + 1) * nv)
            total += jnp.dot(perh[:, lanes], high, preferred_element_type=f32)
            total += jnp.dot(perl[:, lanes], high, preferred_element_type=f32)
            total += jnp.dot(perh[:, lanes], low, preferred_element_type=f32)

    def against(left, right):
        return lax.dot_general(
            left, right, (((1,), (1,)), ((), ())), preferred_element_type=f32
        )

    def sided(slot, source, out):
        mine = total[slot * 4 * cb:(slot + 1) * 4 * cb]
        real = jnp.concatenate([mine[:cb], mine[cb:2 * cb]], axis=1)
        imag = jnp.concatenate([mine[2 * cb:3 * cb], mine[3 * cb:]], axis=1)
        yh, yl = split(jnp.concatenate([real, imag], axis=0))
        uh, ul = split(
            jnp.concatenate([source[0, :, :2 * nv], source[1, :, :2 * nv]], axis=0)
        )
        quads = against(uh, yh) + against(uh, yl) + against(ul, yh)
        zr = quads[:cb, :cb] + quads[cb:, cb:]
        zi = quads[:cb, cb:] - quads[cb:, :cb]
        out[0] = zi - jnp.transpose(zi)
        out[1] = -(zr + jnp.transpose(zr))

    sided(1, pper, res_out)
    got_res = send(res_out, res_in, partner)
    sided(0, per, res_own)

    mine = [rows_of(me, i) for i in range(3)]
    got_rows.wait()
    yours = [[rows_in[i, ri, :rl] for ri in range(2)] for i in range(3)]
    for k in range(3):
        for ri in range(2):
            here = sum(in_dir[k][i] * mine[i][ri] for i in range(3))
            there = sum(in_dir[k][i] * yours[i][ri] for i in range(3))
            by_time = [jnp.where(b == t, here, there) for t in range(2)]
            for g in range(NG):
                elem[g, k, ri] = in_group[g][0] * by_time[0] + in_group[g][1] * by_time[1]
    got_res.wait()
    weight = [jnp.where(b == 0, in_block[0], in_block[1]), jnp.where(b == 0, in_block[1], in_block[0])]
    blocks[...] = weight[0] * res_own[...] + weight[1] * res_in[...]


def body(vectors, links, directions, slice_group, peram, block_group, *, n):
    nt, _, _, sites, nv = vectors.shape
    cb = peram.shape[2]
    lnk = jnp.transpose(links, (0, 1, 3, 4, 2, 5))
    hbm = pl.BlockSpec(memory_space=pltpu.HBM)
    vmem = pl.BlockSpec(memory_space=pltpu.VMEM)
    smem = pl.BlockSpec(memory_space=pltpu.SMEM)
    copies = 64
    row_room = max(nv // n, 8)
    return pl.pallas_call(
        functools.partial(kernel, n),
        out_shape=(
            jax.ShapeDtypeStruct((NG, 3, 2, nv // n, nv), f32),
            jax.ShapeDtypeStruct((2, cb, cb), f32),
        ),
        in_specs=[hbm, hbm, hbm, smem, smem, smem],
        out_specs=(vmem, vmem),
        scratch_shapes=[
            pltpu.VMEM((2, 3, sites, nv), f32),
            pltpu.VMEM((3, 3, 3, 2, sites), f32),
            pltpu.VMEM((2, cb, 4 * nv), f32),
            pltpu.VMEM((2, 3, sites, nv), f32),
            pltpu.VMEM((2, 3, sites, nv), f32),
            pltpu.VMEM((2, 2, 3, LZ, nv), f32),
            pltpu.VMEM((3, 3, 3, 2, sites), f32),
            pltpu.VMEM((3, 3, 3, 2, sites), f32),
            pltpu.VMEM((6, sites, 64), f32),
            pltpu.VMEM((2, CHUNKS, nv, 6 * sites // CHUNKS), bf16),
            pltpu.VMEM((2, CHUNKS, nv, 6 * sites // CHUNKS), bf16),
            pltpu.VMEM((2, 6 * sites // CHUNKS, 2 * nv), bf16),
            pltpu.VMEM((2, 6 * sites // CHUNKS, 2 * nv), bf16),
            pltpu.VMEM((3, nv, 2 * nv), f32),
            pltpu.VMEM((3, nv, nv), f32),
            pltpu.VMEM((3, nv, nv), f32),
            pltpu.VMEM((3, nv, nv), f32),
            pltpu.VMEM((3, 128, nv), f32),
            pltpu.VMEM((8 * cb, 6 * nv), bf16),
            pltpu.VMEM((8 * cb, 6 * nv), bf16),
            pltpu.VMEM((2, cb, 4 * nv), f32),
            pltpu.VMEM((3, 2, row_room, nv), f32),
            pltpu.VMEM((3, 2, row_room, nv), f32),
            pltpu.VMEM((2, cb, cb), f32),
            pltpu.VMEM((2, cb, cb), f32),
            pltpu.VMEM((2, cb, cb), f32),
            pltpu.SemaphoreType.DMA((copies,)),
            pltpu.SemaphoreType.DMA((copies,)),
            pltpu.SemaphoreType.DMA((2, CHUNKS)),
            pltpu.SemaphoreType.DMA((2, CHUNKS)),
            pltpu.SemaphoreType.DMA,
            pltpu.SemaphoreType.DMA,
            pltpu.SemaphoreType.DMA((3,)),
        ],
        compiler_params=pltpu.CompilerParams(
            collective_id=0, has_side_effects=True, vmem_limit_bytes=63 * 2**20
        ),
    )(vectors, lnk, jnp.swapaxes(peram, 1, 2), directions, slice_group, block_group)


def solution(mesh):
    return jax.shard_map(
        functools.partial(body, n=mesh.shape["space"]),
        mesh=mesh,
        in_specs=(
            P("cfg", None, None, "space", None),
            P("cfg", None, None, None, None, "space"),
            P(),
            P(),
            P("cfg", None, "space"),
            P("space"),
        ),
        out_specs=(P("cfg", None, None, "space", None), P("cfg", "space", None)),
        check_vma=False,
    )
```
